128 devices in a mesh: band: 8 (over z, core), strip: 16 (over y, x).
Axes of the slice: x: 4, y: 4, z: 4, core: 2. Of those that a mesh axis runs over, the one named last changes fastest.
Arguments:
- first_scene: bfloat16 [4096, 8192], P('band', 'strip'), may hold values from -6 to 6
- second_scene: bfloat16 [4096, 8192], P('band', 'strip'), may hold values from -6 to 6
- owner_strip: int32 [8, 16, 16, 1], P('band', 'strip'), may hold values from 0 to 15; in each aligned block of 16 rows (0 to 15, 16 to 31, ..., all dimensions but the last counted through in order) at most 2 rows name the same one
- target_tile: int32 [8, 16, 16], P('band', 'strip'), may hold values from 0 to 15
- offsets: int32 [8, 16, 16, 2], P('band', 'strip'), may hold values from -32 to 32
- valid_mask: int32 [8, 16, 16], P('band', 'strip'), may hold values 0 or 1
Outputs:
- consistency: float32 [8, 16, 16, 4096], P('band', 'strip')
The draws below stay inside these ranges and needn't reach their ends.
Inputs may be any that keep to these rules, and one draw needn't show every extreme that they name: `owner_strip`: among the 16 patches of one device at most 2 name the same owner strip, and in every draw some device has 2 patches naming one strip.
All inputs are finite; a program needn't handle non-finite values. No bound on the sum of `valid_mask` on one device may be relied on, other than what follows from the above.
Results may differ from the reference program's by a relative error of at most 0.0003.
Values may be sent and summed in bfloat16 or wider, within the bound.
No kernel may reach another device: no remote copies, remote signals or barrier semaphores. Data moves between devices by JAX's collectives and lax.ppermute only.
A program may use at most 128 MiB of HBM per device.

```python
import math
import jax
import jax.numpy as jnp
import numpy as np
from jax import lax

PATCH_SIDE = 128
SHIFTS = 64
ROW_PATCHES = 4
COL_PATCHES = 4
PATCHES = 16
SEARCH = 192
PADDED = 256
CAPACITY = 2
IMAGE_ROWS = 4096
IMAGE_COLS = 8192
N_BAND = 8
N_STRIP = 16


def place_ends(result, own_key, least, top_value):
    dims = result.shape
    spot = [jax.random.randint(jax.random.fold_in(own_key, axis), (), 0, dims[axis]) for axis in range(len(dims))]
    result = result.at[tuple(spot)].set(least)
    longest = dims.index(max(dims))
    spot[longest] = (spot[longest] + 1) % dims[longest]
    return result.at[tuple(spot)].set(top_value)


def block_scale(key, extent, pieces, low, high):
    def one(position, shards_of):
        steps = jax.random.uniform(jax.random.fold_in(jax.random.fold_in(key, 6), position), (shards_of,), jnp.float32, low / len(pieces), high / len(pieces))
        return jnp.repeat(jnp.exp(steps), extent[position] // shards_of).reshape((-1,) + (1,) * (len(extent) - position - 1))

    level = one(*pieces[0])
    for cut in pieces[1:]:
        level = level * one(*cut)
    return level


def assign_block(key, own, number, rows, number_of, top, limit, lean):
    sequence = jax.random.permutation(key, number_of)
    packed, usual = portions_of(number_of, rows * top, limit, lean, True), portions_of(number_of, rows * top, limit, lean, False)
    places = jnp.arange(number_of)

    def named(tallies, turn):
        used = int((tallies > 0).sum())
        fixed = max(1, used // 4)
        passed = fixed + (places - fixed + turn * (used - fixed)) % max(1, number_of - fixed)
        return jnp.zeros((number_of,), jnp.int32).at[sequence[jnp.where(places < fixed, places, passed)]].set(jnp.asarray(tallies, jnp.int32))

    tallies = jnp.where(number % 4 == 0, named(packed, number // 4), named(usual, number - number // 4 - 1))
    mixed = jax.random.permutation(jax.random.fold_in(own, 3), number_of)
    giver, receiver = mixed[0:number_of // 2 * 2:2], mixed[1:number_of // 2 * 2:2]
    margin = jnp.minimum(tallies[giver] - 1, limit - tallies[receiver]) // 2
    margin = jnp.where((giver == sequence[0]) | (receiver == sequence[0]) | (tallies[receiver] == 0), 0, jnp.maximum(margin, 0))
    passed = jax.random.randint(jax.random.fold_in(own, 4), (number_of // 2,), 0, 1 << 20) % (margin + 1)
    tallies = tallies.at[giver].add(-passed).at[receiver].add(passed)
    labels = jnp.searchsorted(jnp.cumsum(tallies), jnp.arange(rows * top), side="right").astype(jnp.int32)
    listing = labels.reshape(top, rows).T
    listing = listing[jax.random.permutation(jax.random.fold_in(own, 1), rows)]
    turn = jax.random.randint(jax.random.fold_in(own, 2), (rows, 1), 0, top)
    return jnp.take_along_axis(listing, (jnp.arange(top)[None, :] + turn) % top, axis=1)


def portions_of(number_of, total, bound, slope, full):
    weights = [(1 << 20) // math.isqrt(standing ** slope) + 1 for standing in range(1, number_of + 1)]
    largest = bound if full else min(bound, max(-(-total // number_of), total * weights[0] // sum(weights)))
    least = 1 if total - largest >= number_of - 1 else 0
    given, spare = [largest] + [least] * (number_of - 1), total - largest - least * (number_of - 1)
    while spare > 0:
        movable = [i for i in range(1, number_of) if given[i] < largest] or [i for i in range(1, number_of) if given[i] < bound]
        whole, remaining = sum([weights[i] for i in movable]), spare
        for i in movable:
            more = min(bound - given[i], max(1, remaining * weights[i] // whole), spare)
            given[i] = given[i] + more
            spare = spare - more
    return np.array(given)


def noise(key, shape, spread, bound, pieces=(), held_as=jnp.bfloat16):
    gain = block_scale(key, shape, pieces, -0.22, 0.18) if pieces else 1.0
    values = jax.random.normal(key, shape, jnp.float32) * spread * gain
    return jnp.minimum(jnp.maximum(values, -bound), bound).astype(held_as)


def setup_inputs(seed: int = 0) -> dict:
    key_list = jax.random.split(jax.random.key(seed), 7)
    first_scene = noise(key_list[0], (IMAGE_ROWS, IMAGE_COLS), 1.0, 6.0, ((0, 8), (1, 16)))
    second_scene = noise(key_list[1], (IMAGE_ROWS, IMAGE_COLS), 1.0, 6.0, ((0, 8), (1, 16)))
    owner_strip_keys = jax.random.split(jax.random.fold_in(key_list[2], 1), N_BAND * N_STRIP * PATCHES // PATCHES)
    owner_strip_turns = jax.random.permutation(jax.random.fold_in(key_list[2], 3), N_BAND * N_STRIP * PATCHES // PATCHES)
    owner_strip = jax.vmap(lambda own, number: assign_block(jax.random.fold_in(key_list[2], 2), own, number, PATCHES, N_STRIP, 1, CAPACITY, 2))(owner_strip_keys, owner_strip_turns).reshape((N_BAND, N_STRIP, PATCHES, 1))
    target_tile = place_ends(jax.random.randint(key_list[3], (N_BAND, N_STRIP, PATCHES), 0, PATCHES), jax.random.fold_in(key_list[3], 1), 0, PATCHES - 1).astype(jnp.int32)
    offsets = place_ends(jax.random.randint(key_list[4], (N_BAND, N_STRIP, PATCHES, 2), 0 - SHIFTS // 2, SHIFTS // 2 + 1), jax.random.fold_in(key_list[4], 1), 0 - SHIFTS // 2, (SHIFTS // 2 + 1) - 1).astype(jnp.int32)
    valid_mask = place_ends((jax.random.randint(key_list[5], (N_BAND, N_STRIP, PATCHES), 0, 4) < 3).astype(jnp.int32), jax.random.fold_in(key_list[5], 1), 0, 1)
    return dict(first_scene=first_scene, second_scene=second_scene, owner_strip=owner_strip, target_tile=target_tile, offsets=offsets, valid_mask=valid_mask)


EPSILON = 1e-05

def normalize(patch):
    centered = patch - jnp.mean(patch)
    return centered * lax.rsqrt(jnp.mean(centered * centered) + EPSILON)

def correlate(template, window):
    spec_template = jnp.fft.rfft2(template, s=(PADDED, PADDED))
    spec_window = jnp.fft.rfft2(window, s=(PADDED, PADDED))
    surface = jnp.fft.irfft2(jnp.conj(spec_template) * spec_window, s=(PADDED, PADDED))
    return surface[:SHIFTS, :SHIFTS]

def reference(first_scene, second_scene, owner_strip, target_tile, offsets, valid_mask):
    middle = SHIFTS // 2
    padded_first = jnp.pad(first_scene, SHIFTS)
    padded_second = jnp.pad(second_scene, SHIFTS)
    patch_total = N_BAND * N_STRIP * PATCHES
    owners = owner_strip.reshape(patch_total).astype(jnp.int32)
    tile_list = target_tile.reshape(patch_total).astype(jnp.int32)
    shifts = offsets.reshape(patch_total, 2).astype(jnp.int32)
    mask_list = valid_mask.reshape(patch_total)
    indices = jnp.arange(patch_total, dtype=jnp.int32)

    def one_patch(inputs):
        patch_index, strip_owner, tile_index, fine_shift, keep_flag = inputs
        band_index = patch_index // (N_STRIP * PATCHES)
        strip_index = patch_index // PATCHES % N_STRIP
        local_index = patch_index % PATCHES
        patch_top = (band_index * ROW_PATCHES + local_index // COL_PATCHES) * PATCH_SIDE
        patch_left = (strip_index * COL_PATCHES + local_index % COL_PATCHES) * PATCH_SIDE
        target_top = (band_index * ROW_PATCHES + tile_index // COL_PATCHES) * PATCH_SIDE
        target_left = (strip_owner * COL_PATCHES + tile_index % COL_PATCHES) * PATCH_SIDE
        search = lax.dynamic_slice(padded_second, ((target_top + fine_shift[0] - middle + SHIFTS).astype(jnp.int32), (target_left + fine_shift[1] - middle + SHIFTS).astype(jnp.int32)), (SEARCH, SEARCH)).astype(jnp.float32)
        beside_all = lax.dynamic_slice(padded_first, ((patch_top - middle + 1 + SHIFTS).astype(jnp.int32), (patch_left - middle + 1 + SHIFTS).astype(jnp.int32)), (SEARCH, SEARCH)).astype(jnp.float32)
        template = normalize(beside_all[middle - 1:middle - 1 + PATCH_SIDE, middle - 1:middle - 1 + PATCH_SIDE])
        backward = normalize(search[middle:middle + PATCH_SIDE, middle:middle + PATCH_SIDE])
        forward_surface = correlate(template, search)
        backward_surface = correlate(backward, beside_all)
        combined = (forward_surface + backward_surface[::-1, ::-1]) / (2.0 * PATCH_SIDE)
        return (combined * keep_flag.astype(jnp.float32)).reshape(SHIFTS * SHIFTS)
    surfaces = lax.map(one_patch, (indices, owners, tile_list, shifts, mask_list))
    return surfaces.reshape(N_BAND, N_STRIP, PATCHES, SHIFTS * SHIFTS)
```

```python
import jax
import jax.numpy as jnp
from jax import lax
from jax.experimental import pallas as pl
from jax.experimental.pallas import tpu as pltpu
from jax.sharding import PartitionSpec as P

SIDE = 128
SHIFTS = 64
SEARCH = 192
HALO = 64
EPSILON = 1e-05
COLS = 22
BANDS = 3
ROWS = 16
SPAN = 80
BLOCKS = SIDE // ROWS
DEPTH = BLOCKS * SIDE + 256
PACKED = SEARCH + SEARCH // 2
EXTRA = 32
TALL = COLS * ROWS + EXTRA
DIMS = (((1,), (1,)), ((), ()))


def lane_iota(shape):
    return lax.broadcasted_iota(jnp.int32, shape, len(shape) - 1)


def cut_kernel(requests, scene_ref, out_ref, wide):
    for part in range(5):
        wide[part] = scene_ref[:, 128 * part : 128 * (part + 1)].astype(jnp.float32)
    wide[5] = jnp.zeros((640, 128), jnp.float32)
    lanes = lane_iota((SEARCH, 128))
    lower = lane_iota((SEARCH // 2, 128)) < 64

    def one(slot, carry):
        top = requests[slot // 2, slot % 2, 0]
        left = requests[slot // 2, slot % 2, 1]
        base = left // 128
        rest = left % 128
        turn = (128 - rest) % 128
        turned = [
            pltpu.roll(wide[base + part, pl.ds(top, SEARCH), :], turn, 1) for part in range(3)
        ]
        inside = lanes < 128 - rest
        near = jnp.where(inside, turned[0], turned[1])
        far = jnp.where(inside, turned[1], turned[2])
        out_ref[slot, :SEARCH, :] = near.astype(jnp.bfloat16)
        half = SEARCH // 2
        mixed = jnp.where(lower, far[:half], pltpu.roll(far[half:], 64, 1))
        out_ref[slot, SEARCH:, :] = mixed.astype(jnp.bfloat16)
        return carry

    lax.fori_loop(0, out_ref.shape[0], one, 0)


def cut_windows(scene, requests):
    slots = 2 * requests.shape[0]
    return pl.pallas_call(
        cut_kernel,
        out_shape=jax.ShapeDtypeStruct((slots, PACKED, 128), jnp.bfloat16),
        in_specs=[
            pl.BlockSpec(memory_space=pltpu.SMEM),
            pl.BlockSpec(memory_space=pltpu.VMEM),
        ],
        out_specs=pl.BlockSpec(memory_space=pltpu.VMEM),
        scratch_shapes=[pltpu.VMEM((6, 640, 128), jnp.float32)],
        compiler_params=pltpu.CompilerParams(vmem_limit_bytes=32 * 1024 * 1024),
        name="cut_windows",
    )(requests, scene)


def normalize(patch):
    centered = patch - jnp.mean(patch)
    return centered * lax.rsqrt(jnp.mean(centered * centered) + EPSILON)


def exchange(size):
    rows = lax.broadcasted_iota(jnp.int32, (size, size), 0)
    return (rows + lane_iota((size, size)) == size - 1).astype(jnp.bfloat16)


def halves(values):
    high = values.astype(jnp.bfloat16)
    low = (values - high.astype(jnp.float32)).astype(jnp.bfloat16)
    return high, low


def spread_template(values, left, row_at, lane_at, reverse):
    lanes = lane_iota((ROWS, 128)).astype(jnp.int16)
    groups = (lane_iota((ROWS, 128)) // 32).astype(jnp.int16)
    within = (lane_iota((ROWS, 128)) % 32).astype(jnp.int16)
    zero = jnp.zeros((ROWS, 128), jnp.bfloat16)
    blocks = [values[ROWS * q : ROWS * (q + 1)] for q in range(BLOCKS)]
    ends = []
    for group in range(2):
        end = zero
        for part in range(4):
            turned = pltpu.roll(blocks[4 * group + part], 32 * part, 1)
            end = jnp.where(groups == (part + 3) % 4, turned, end)
        ends.append(end)
    for a in range(COLS):
        shift = COLS - 1 - a if reverse else a
        rows = pl.ds(row_at + ROWS * a, ROWS)
        for q in range(BLOCKS):
            moved = pltpu.roll(blocks[q], shift, 1)
            moved = jnp.where(lanes >= shift, moved, zero)
            left[rows, pl.ds(lane_at + 128 * q, 128)] = moved
        for group in range(2):
            moved = pltpu.roll(ends[group], shift, 1)
            moved = jnp.where(within < shift, moved, zero)
            left[rows, pl.ds(lane_at + 128 * (BLOCKS + group), 128)] = moved


def spread_window(near, far, right, lane_at, offsets):
    lanes = lane_iota((SEARCH, 128)).astype(jnp.int16)
    for b, offset in enumerate(offsets):
        back = (128 - offset) % 128
        main = near
        if offset:
            main = jnp.where(
                lanes < 128 - offset, pltpu.roll(near, back, 1), pltpu.roll(far, back, 1)
            )
        rows = pl.ds(SPAN * b, SPAN)
        for q in range(BLOCKS):
            right[rows, pl.ds(lane_at + 128 * q, 128)] = main[ROWS * q : ROWS * q + SPAN]
        turned = [pltpu.roll(far, (back + 32 * part) % 128, 1) for part in range(4)]
        few = (lane_iota((SPAN, 128)) // 32).astype(jnp.int16)
        for group in range(2):
            tail = turned[0][ROWS * 4 * group : ROWS * 4 * group + SPAN]
            for part in range(1, 4):
                q = 4 * group + part
                tail = jnp.where(few == part, turned[part][ROWS * q : ROWS * q + SPAN], tail)
            right[rows, pl.ds(lane_at + 128 * (BLOCKS + group), 128)] = tail


def fold_diagonals(product):
    cube = product.reshape(COLS, ROWS, 256)
    level = lax.broadcasted_iota(jnp.int32, (COLS * 8, 256), 0) % 8
    part = cube[:, :8].reshape(COLS * 8, 256) + pltpu.roll(
        cube[:, 8:].reshape(COLS * 8, 256), 248, 1
    )
    for bit in (4, 2, 1):
        part = jnp.where(level & bit != 0, pltpu.roll(part, 256 - bit, 1), part)
    return jnp.sum(part.reshape(COLS, 8, 256), axis=1)


def search_block(windows_ref, slot):
    near = windows_ref[slot, :SEARCH, :]
    packed = windows_ref[slot, SEARCH:, :]
    return near, jnp.concatenate([packed, pltpu.roll(packed, 64, 1)], axis=0)


def flipped_centre(near, far):
    flip = exchange(128)
    low, high = [
        jnp.dot(flip, part[32:160], preferred_element_type=jnp.float32) for part in (near, far)
    ]
    lanes = lane_iota((128, 128))
    return jnp.where(lanes < 96, pltpu.roll(low, 96, 1), pltpu.roll(high, 96, 1))


def flipped_around(beside_ref, row, col):
    return jnp.dot(
        exchange(SEARCH),
        beside_ref[pl.ds(row + 32, SEARCH), pl.ds(col, 256)],
        preferred_element_type=jnp.float32,
    ).astype(jnp.bfloat16)


def place_of(patch):
    return pl.multiple_of(patch // 4 * 128, 128), pl.multiple_of(patch % 4 * 128, 128)


def careful_kernel(slots, first_ref, beside_ref, windows_ref, out_ref, left, right):
    right[SPAN * BANDS :, :] = jnp.zeros((256 - SPAN * BANDS, 2 * DEPTH), jnp.bfloat16)
    count = COLS * ROWS

    def one(patch, carry):
        row, col = place_of(patch)
        near, far = search_block(windows_ref, slots[patch])
        template = normalize(first_ref[pl.ds(row, 128), pl.ds(col, 128)].astype(jnp.float32))
        centre = flipped_centre(near, far)
        around = flipped_around(beside_ref, row, col)
        inner = first_ref[pl.ds(row, 128), pl.ds(col, 128)].astype(jnp.float32)
        sides = ((template, jnp.mean(centre), False), (normalize(centre), jnp.mean(inner), True))
        rest = jnp.float32(0.0)
        for place, (values, level, reverse) in enumerate(sides):
            high, low = halves(values)
            for half, piece in enumerate((high, low)):
                spread_template(piece, left, count * half, DEPTH * place, reverse)
            rest += level * (
                jnp.sum(high.astype(jnp.float32)) + jnp.sum(low.astype(jnp.float32))
            )
        spread_window(near, far, right, 0, (0, 22, 44))
        spread_window(around[:, :128], around[:, 128:], right, DEPTH, (75, 53, 31))
        both = lax.dot_general(left[...], right[...], DIMS, preferred_element_type=jnp.float32)
        out_ref[patch] = fold_diagonals(both[:count] + both[count:]) - rest
        return carry

    lax.fori_loop(0, 16, one, 0)


def careful_surfaces(slots, first, beside, windows):
    return pl.pallas_call(
        careful_kernel,
        out_shape=jax.ShapeDtypeStruct((16, COLS, 256), jnp.float32),
        in_specs=[pl.BlockSpec(memory_space=pltpu.SMEM)]
        + [pl.BlockSpec(memory_space=pltpu.VMEM)] * 3,
        out_specs=pl.BlockSpec(memory_space=pltpu.VMEM),
        scratch_shapes=[
            pltpu.VMEM((2 * COLS * ROWS, 2 * DEPTH), jnp.bfloat16),
            pltpu.VMEM((256, 2 * DEPTH), jnp.bfloat16),
        ],
        compiler_params=pltpu.CompilerParams(vmem_limit_bytes=40 * 1024 * 1024),
        name="careful_surfaces",
    )(slots, first, beside, windows)


def ones_rows(left, reverse):
    index = lax.broadcasted_iota(jnp.int32, (EXTRA, 128), 0)
    lanes = lane_iota((EXTRA, 128))
    shift = COLS - 1 - index if reverse else index
    main = jnp.where((index < COLS) & (lanes >= shift), 1.0, 0.0).astype(jnp.bfloat16)
    tail = jnp.where((index < COLS) & (lanes % 32 < shift), 1.0, 0.0).astype(jnp.bfloat16)
    for q in range(BLOCKS):
        left[COLS * ROWS :, 128 * q : 128 * (q + 1)] = main
    for group in range(2):
        at = 128 * (BLOCKS + group)
        left[COLS * ROWS :, at : at + 128] = tail


def level_of(values):
    mean = jnp.mean(values)
    centered = values - mean
    spread = jnp.mean(centered * centered)
    large = jnp.where(mean * mean > 4.0 * spread, 1.0, 0.0)
    return mean, lax.rsqrt(jnp.full((1, 256), spread + EPSILON)), large


def prepare_kernel(first_ref, beside_ref, left_out, right_out, level_out):
    row, col = place_of(pl.program_id(0))
    left, right = left_out.at[0], right_out.at[0]
    tile = first_ref[pl.ds(row, 128), pl.ds(col, 128)]
    mean, scale, large = level_of(tile.astype(jnp.float32))
    level_out[0, 0:1, :] = scale * mean
    level_out[0, 1:2, :] = scale
    level_out[0, 2:3, :] = jnp.full((1, 256), large)
    level_out[0, 3:8, :] = jnp.zeros((5, 256), jnp.float32)
    spread_template(tile, left, 0, 0, False)
    ones_rows(left, False)
    around = flipped_around(beside_ref, row, col)
    spread_window(around[:, :128], around[:, 128:], right, 0, (75, 53, 31))
    right[SPAN * BANDS :, :] = jnp.zeros((256 - SPAN * BANDS, DEPTH), jnp.bfloat16)


def prepared(first, beside):
    whole = pl.BlockSpec(memory_space=pltpu.VMEM)
    shapes = ((TALL, DEPTH, jnp.bfloat16), (256, DEPTH, jnp.bfloat16), (8, 256, jnp.float32))
    return pl.pallas_call(
        prepare_kernel,
        grid=(16,),
        out_shape=[pltpu.HBM((16, m, n), kind) for m, n, kind in shapes],
        in_specs=[whole, whole],
        out_specs=[pl.BlockSpec((1, m, n), lambda k: (k, 0, 0)) for m, n, _ in shapes],
        compiler_params=pltpu.CompilerParams(vmem_limit_bytes=24 * 1024 * 1024),
        cost_estimate=pl.CostEstimate(
            flops=20_000_000_000, bytes_accessed=30_000_000, transcendentals=0
        ),
        name="prepare",
    )(first, beside)


def surface_kernel(
    slots, windows_ref, left_ref, right_ref, level_ref, out_ref, large_ref, *scratch
):
    step = pl.program_id(0)
    count = COLS * ROWS

    @pl.when(step == 0)
    def _():
        large_ref[0] = 0
        for left, right, side in (scratch[:3], scratch[3:]):
            right[SPAN * BANDS :, :] = jnp.zeros((256 - SPAN * BANDS, DEPTH), jnp.bfloat16)
            ones_rows(left, True)

    def both(building, using):
        left, right, side = using
        ahead = lax.dot_general(left_ref[0], right[...], DIMS, preferred_element_type=jnp.float32)
        behind = lax.dot_general(left[...], right_ref[0], DIMS, preferred_element_type=jnp.float32)
        raw = level_ref[0, 1:2, :] * ahead[:count] + side[1:2, :] * behind[:count]
        box = level_ref[0, 0:1, :] * ahead[count:] + side[0:1, :] * behind[count:]
        for shift in (1, 2, 4, 8):
            box = box + pltpu.roll(box, 256 - shift, 1)
        out_ref[0] = fold_diagonals(raw) - box[:COLS]

        left, right, side = building
        near, far = search_block(windows_ref, slots[jnp.minimum(step, 15)])
        centre = flipped_centre(near, far)
        spread_window(near, far, right, 0, (0, 22, 44))
        spread_template(centre.astype(jnp.bfloat16), left, 0, 0, True)
        mean, scale, large = level_of(centre)
        side[0:1, :] = scale * mean
        side[1:2, :] = scale
        large_ref[0] = jnp.maximum(
            large_ref[0], jnp.maximum(large, jnp.max(level_ref[0, 2:3, :])).astype(jnp.int32)
        )

    @pl.when(step % 2 == 0)
    def _():
        both(scratch[:3], scratch[3:])

    @pl.when(step % 2 == 1)
    def _():
        both(scratch[3:], scratch[:3])


def surfaces_of(slots, windows, left, right, level):
    def block(m, n):
        return pl.BlockSpec((1, m, n), lambda k: (jnp.maximum(k - 1, 0), 0, 0))

    return pl.pallas_call(
        surface_kernel,
        grid=(17,),
        out_shape=[
            jax.ShapeDtypeStruct((16, COLS, 256), jnp.float32),
            jax.ShapeDtypeStruct((1,), jnp.int32),
        ],
        in_specs=[
            pl.BlockSpec(memory_space=pltpu.SMEM),
            pl.BlockSpec(memory_space=pltpu.VMEM),
            block(TALL, DEPTH),
            block(256, DEPTH),
            block(8, 256),
        ],
        out_specs=[block(COLS, 256), pl.BlockSpec(memory_space=pltpu.SMEM)],
        scratch_shapes=[
            pltpu.VMEM((TALL, DEPTH), jnp.bfloat16),
            pltpu.VMEM((256, DEPTH), jnp.bfloat16),
            pltpu.VMEM((8, 256), jnp.float32),
        ]
        * 2,
        compiler_params=pltpu.CompilerParams(vmem_limit_bytes=24 * 1024 * 1024),
        cost_estimate=pl.CostEstimate(
            flops=20_000_000_000, bytes_accessed=30_000_000, transcendentals=0
        ),
        name="surfaces",
    )(slots, windows, left, right, level)


def combined(slots, first, beside, windows, ready):
    ready = [pltpu.with_memory_space_constraint(array, pltpu.HBM) for array in ready]
    folded, large = surfaces_of(slots, windows, *ready)
    return lax.cond(
        large[0] > 0,
        lambda: careful_surfaces(slots, first, beside, windows),
        lambda: folded,
    )


def finish(folded, mask):
    parts = folded[:, :, : SPAN * BANDS].reshape(16, COLS, BANDS, SPAN)[..., :SHIFTS]
    surface = parts.transpose(0, 3, 2, 1).reshape(16, SHIFTS, BANDS * COLS)[:, :, :SHIFTS]
    scale = mask.reshape(16, 1).astype(jnp.float32) / (2.0 * SIDE)
    return surface.reshape(16, SHIFTS * SHIFTS) * scale


def moved(values, axis, forward):
    count = lax.axis_size(axis)
    pairs = [(i, i + 1) if forward else (i + 1, i) for i in range(count - 1)]
    return lax.ppermute(values, axis, pairs)


def rows_around(first, second):
    from_above = moved(jnp.concatenate([first[-HALO:], second[-HALO:]], 1), "band", True)
    from_below = moved(jnp.concatenate([first[:HALO], second[:HALO]], 1), "band", False)
    return from_above, from_below


def with_margins(first, second, from_above, from_below):
    width = first.shape[1]
    first = jnp.concatenate([from_above[:, :width], first, from_below[:, :width]], 0)
    second = jnp.concatenate([from_above[:, width:], second, from_below[:, width:]], 0)
    from_left = moved(jnp.concatenate([first[:, -HALO:], second[:, -HALO:]], 1), "strip", True)
    from_right = moved(jnp.concatenate([first[:, :HALO], second[:, :HALO]], 1), "strip", False)
    first = jnp.concatenate([from_left[:, :HALO], first, from_right[:, :HALO]], 1)
    second = jnp.concatenate([from_left[:, HALO:], second, from_right[:, HALO:]], 1)
    return first, second


def to_owners(values):
    return lax.all_to_all(values, "strip", split_axis=0, concat_axis=0, tiled=True)


def on_device(first, second, owner_strip, target_tile, offsets, valid_mask):
    strips = lax.axis_size("strip")
    from_above, from_below = rows_around(first, second)
    order = jnp.arange(16, dtype=jnp.int32)
    owners = owner_strip.reshape(16)
    earlier = (owners[:, None] == owners[None, :]) & (order[None, :] < order[:, None])
    slot_of = owners * 2 + jnp.sum(earlier.astype(jnp.int32), axis=1)
    placing = (slot_of[:, None] == jnp.arange(2 * strips, dtype=jnp.int32)[None, :]).astype(jnp.int32)
    tiles = target_tile.reshape(16)
    shifts = offsets.reshape(16, 2)
    corner = jnp.stack(
        [tiles // 4 * SIDE + shifts[:, 0] + 32, tiles % 4 * SIDE + shifts[:, 1] + 32], axis=1
    )
    outgoing = jnp.sum(placing[:, :, None] * corner[:, None, :], axis=0).reshape(strips, 2, 2)
    outgoing, from_above, from_below = lax.optimization_barrier((outgoing, from_above, from_below))
    requests = to_owners(outgoing)
    beside, wide = with_margins(first, second, from_above, from_below)
    windows = cut_windows(wide, requests)
    windows = to_owners(windows.reshape(strips, 2 * PACKED, 128))
    windows = windows.reshape(2 * strips, PACKED, 128)
    folded = combined(slot_of, first, beside, windows, prepared(first, beside))
    return finish(folded, valid_mask).reshape(1, 1, 16, SHIFTS * SHIFTS)


def bench(slots, first, beside, windows, mask):
    return finish(combined(slots, first, beside, windows, prepared(first, beside)), mask)


def solution(mesh):
    return jax.shard_map(
        on_device,
        mesh=mesh,
        in_specs=(
            P("band", "strip"),
            P("band", "strip"),
            P("band", "strip", None, None),
            P("band", "strip", None),
            P("band", "strip", None, None),
            P("band", "strip", None),
        ),
        out_specs=P("band", "strip", None, None),
        check_vma=False,
    )
```

```python
import functools

import jax
import jax.numpy as jnp
from jax import lax
from jax.experimental import pallas as pl
from jax.experimental.pallas import tpu as pltpu
from jax.sharding import PartitionSpec as P

SIDE = 128
SHIFTS = 64
SEARCH = 192
HALO = 64
EPSILON = 1e-05
COLS = 22
BANDS = 3
ROWS = 16
SPAN = 80
BLOCKS = SIDE // ROWS
DEPTH = BLOCKS + 2
PACKED = SEARCH + SEARCH // 2
EXTRA = 32
TALL = COLS * ROWS + EXTRA
DIMS = (((1,), (1,)), ((), ()))


def lane_iota(shape):
    return lax.broadcasted_iota(jnp.int32, shape, len(shape) - 1)


def cut_kernel(requests, scene_ref, out_ref, wide, *, place):
    for part in range(5):
        wide[part] = scene_ref[:, 128 * part : 128 * (part + 1)].astype(jnp.float32)
    wide[5] = jnp.zeros((640, 128), jnp.float32)
    lanes = lane_iota((SEARCH, 128))
    lower = lane_iota((SEARCH // 2, 128)) < 64

    def one(slot, carry):
        top = requests[slot, place, 0]
        left = requests[slot, place, 1]
        base = left // 128
        rest = left % 128
        turn = (128 - rest) % 128
        turned = [
            pltpu.roll(wide[base + part, pl.ds(top, SEARCH), :], turn, 1) for part in range(3)
        ]
        inside = lanes < 128 - rest
        near = jnp.where(inside, turned[0], turned[1])
        far = jnp.where(inside, turned[1], turned[2])
        out_ref[slot, :SEARCH, :] = near.astype(jnp.bfloat16)
        half = SEARCH // 2
        mixed = jnp.where(lower, far[:half], pltpu.roll(far[half:], 64, 1))
        out_ref[slot, SEARCH:, :] = mixed.astype(jnp.bfloat16)
        return carry

    lax.fori_loop(0, out_ref.shape[0], one, 0)


def cut_windows(scene, requests, place):
    slots = requests.shape[0]
    return pl.pallas_call(
        functools.partial(cut_kernel, place=place),
        out_shape=jax.ShapeDtypeStruct((slots, PACKED, 128), jnp.bfloat16),
        in_specs=[
            pl.BlockSpec(memory_space=pltpu.SMEM),
            pl.BlockSpec(memory_space=pltpu.VMEM),
        ],
        out_specs=pl.BlockSpec(memory_space=pltpu.VMEM),
        scratch_shapes=[pltpu.VMEM((6, 640, 128), jnp.float32)],
        compiler_params=pltpu.CompilerParams(vmem_limit_bytes=32 * 1024 * 1024),
        name="cut_windows",
    )(requests, scene)


def normalize(patch):
    centered = patch - jnp.mean(patch)
    return centered * lax.rsqrt(jnp.mean(centered * centered) + EPSILON)


def exchange(size):
    rows = lax.broadcasted_iota(jnp.int32, (size, size), 0)
    return (rows + lane_iota((size, size)) == size - 1).astype(jnp.bfloat16)


def halves(values):
    high = values.astype(jnp.bfloat16)
    low = (values - high.astype(jnp.float32)).astype(jnp.bfloat16)
    return high, low


def spread_template(values, left, row_at, lane_at, reverse):
    lanes = lane_iota((ROWS, 128)).astype(jnp.int16)
    groups = (lane_iota((ROWS, 128)) // 32).astype(jnp.int16)
    within = (lane_iota((ROWS, 128)) % 32).astype(jnp.int16)
    zero = jnp.zeros((ROWS, 128), jnp.bfloat16)
    blocks = [values[ROWS * q : ROWS * (q + 1)] for q in range(BLOCKS)]
    ends = []
    for group in range(2):
        end = zero
        for part in range(4):
            turned = pltpu.roll(blocks[4 * group + part], 32 * part, 1)
            end = jnp.where(groups == (part + 3) % 4, turned, end)
        ends.append(end)
    for a in range(COLS):
        shift = COLS - 1 - a if reverse else a
        rows = pl.ds(row_at + ROWS * a, ROWS)
        for q in range(BLOCKS):
            moved = pltpu.roll(blocks[q], shift, 1)
            moved = jnp.where(lanes >= shift, moved, zero)
            left[lane_at + q, rows] = moved
        for group in range(2):
            moved = pltpu.roll(ends[group], shift, 1)
            moved = jnp.where(within < shift, moved, zero)
            left[lane_at + BLOCKS + group, rows] = moved


def spread_window(near, far, right, lane_at, offsets):
    lanes = lane_iota((SEARCH, 128)).astype(jnp.int16)
    for b, offset in enumerate(offsets):
        back = (128 - offset) % 128
        main = near
        if offset:
            main = jnp.where(
                lanes < 128 - offset, pltpu.roll(near, back, 1), pltpu.roll(far, back, 1)
            )
        rows = pl.ds(SPAN * b, SPAN)
        for q in range(BLOCKS):
            right[lane_at + q, rows] = main[ROWS * q : ROWS * q + SPAN]
        turned = [pltpu.roll(far, (back + 32 * part) % 128, 1) for part in range(4)]
        few = (lane_iota((SPAN, 128)) // 32).astype(jnp.int16)
        for group in range(2):
            tail = turned[0][ROWS * 4 * group : ROWS * 4 * group + SPAN]
            for part in range(1, 4):
                q = 4 * group + part
                tail = jnp.where(few == part, turned[part][ROWS * q : ROWS * q + SPAN], tail)
            right[lane_at + BLOCKS + group, rows] = tail


def fold_diagonals(product, hold):
    for half in range(2):
        hold[half, : COLS * ROWS] = product[:, 128 * half : 128 * (half + 1)]
    groups = []
    for group in range(3):
        terms = [
            jnp.concatenate(
                [hold[half, pl.ds(128 * group + p, 8, stride=ROWS), :] for half in range(2)], axis=1
            )
            for p in range(ROWS)
        ]
        for step in (8, 4, 2, 1):
            terms = [terms[p] + pltpu.roll(terms[p + step], 256 - step, 1) for p in range(step)]
        groups.append(terms[0])
    return jnp.concatenate(groups, axis=0)


def multiplied(left, right):
    factors = [
        jnp.concatenate([side[block] for block in range(side.shape[0])], axis=1)
        for side in (left, right)
    ]
    return lax.dot_general(*factors, DIMS, preferred_element_type=jnp.float32)


def search_block(windows_ref, slot):
    near = windows_ref[slot, :SEARCH, :]
    packed = windows_ref[slot, SEARCH:, :]
    return near, jnp.concatenate([packed, pltpu.roll(packed, 64, 1)], axis=0)


def flipped_centre(near, far):
    flip = exchange(128)
    low, high = [
        jnp.dot(flip, part[32:160], preferred_element_type=jnp.float32) for part in (near, far)
    ]
    lanes = lane_iota((128, 128))
    return jnp.where(lanes < 96, pltpu.roll(low, 96, 1), pltpu.roll(high, 96, 1))


def flipped_around(beside_ref, row, col):
    return jnp.dot(
        exchange(SEARCH),
        beside_ref[pl.ds(row + 32, SEARCH), pl.ds(col, 256)],
        preferred_element_type=jnp.float32,
    ).astype(jnp.bfloat16)


def place_of(patch):
    return pl.multiple_of(patch // 4 * 128, 128), pl.multiple_of(patch % 4 * 128, 128)


def careful_kernel(owners, later, first_ref, beside_ref, windows_ref, others_ref, out_ref, left, right, hold):
    right[:, SPAN * BANDS :] = jnp.zeros((2 * DEPTH, 256 - SPAN * BANDS, 128), jnp.bfloat16)
    count = COLS * ROWS

    hold[:, count:] = jnp.zeros((2, 32, 128), jnp.float32)
    out_ref[16] = jnp.zeros((24, 256), jnp.float32)

    def one(patch, carry):
        row, col = place_of(patch)
        near, far = [
            jnp.where(later[patch] > 0, other, one)
            for one, other in zip(
                search_block(windows_ref, owners[patch]), search_block(others_ref, owners[patch])
            )
        ]
        template = normalize(first_ref[pl.ds(row, 128), pl.ds(col, 128)].astype(jnp.float32))
        centre = flipped_centre(near, far)
        around = flipped_around(beside_ref, row, col)
        inner = first_ref[pl.ds(row, 128), pl.ds(col, 128)].astype(jnp.float32)
        sides = ((template, jnp.mean(centre), False), (normalize(centre), jnp.mean(inner), True))
        rest = jnp.float32(0.0)
        for place, (values, level, reverse) in enumerate(sides):
            high, low = halves(values)
            for half, piece in enumerate((high, low)):
                spread_template(piece, left, count * half, DEPTH * place, reverse)
            rest += level * (
                jnp.sum(high.astype(jnp.float32)) + jnp.sum(low.astype(jnp.float32))
            )
        spread_window(near, far, right, 0, (0, 22, 44))
        spread_window(around[:, :128], around[:, 128:], right, DEPTH, (75, 53, 31))
        both = multiplied(left, right)
        out_ref[patch] = fold_diagonals(both[:count] + both[count:], hold) - rest
        return carry

    lax.fori_loop(0, 16, one, 0)


def careful_surfaces(owners, later, first, beside, windows, others):
    return pl.pallas_call(
        careful_kernel,
        out_shape=jax.ShapeDtypeStruct((17, 24, 256), jnp.float32),
        in_specs=[pl.BlockSpec(memory_space=pltpu.SMEM)] * 2
        + [pl.BlockSpec(memory_space=pltpu.VMEM)] * 4,
        out_specs=pl.BlockSpec(memory_space=pltpu.VMEM),
        scratch_shapes=[
            pltpu.VMEM((2 * DEPTH, 2 * COLS * ROWS, 128), jnp.bfloat16),
            pltpu.VMEM((2 * DEPTH, 256, 128), jnp.bfloat16),
            pltpu.VMEM((2, 384, 128), jnp.float32),
        ],
        compiler_params=pltpu.CompilerParams(vmem_limit_bytes=40 * 1024 * 1024),
        name="careful_surfaces",
    )(owners, later, first, beside, windows, others)


def ones_rows(left, reverse):
    index = lax.broadcasted_iota(jnp.int32, (EXTRA, 128), 0)
    lanes = lane_iota((EXTRA, 128))
    shift = COLS - 1 - index if reverse else index
    main = jnp.where((index < COLS) & (lanes >= shift), 1.0, 0.0).astype(jnp.bfloat16)
    tail = jnp.where((index < COLS) & (lanes % 32 < shift), 1.0, 0.0).astype(jnp.bfloat16)
    for q in range(BLOCKS):
        left[q, COLS * ROWS :] = main
    for group in range(2):
        left[BLOCKS + group, COLS * ROWS :] = tail


def level_of(values):
    mean = jnp.mean(values)
    centered = values - mean
    spread = jnp.mean(centered * centered)
    large = jnp.where(mean * mean > 4.0 * spread, 1.0, 0.0)
    return mean, lax.rsqrt(jnp.full((1, 256), spread + EPSILON)), large


def surface_kernel(
    owners, turns, count_of, first_ref, beside_ref, windows_ref, *rest, phase
):
    before, (out_ref, large_ref, *scratch) = (rest[0], rest[1:]) if phase else (None, rest)
    count = COLS * ROWS
    large_ref[0] = 0
    if phase:
        out_ref[...] = before[...]
    for ahead, behind, front, back, side, hold in (scratch[:6], scratch[6:]):
        hold[:, count:] = jnp.zeros((2, 32, 128), jnp.float32)
        ones_rows(front, False)
        ones_rows(back, True)
        for right in (ahead, behind):
            right[:, SPAN * BANDS :] = jnp.zeros((DEPTH, 256 - SPAN * BANDS, 128), jnp.bfloat16)

    def build(index, buffers):
        ahead, behind, front, back, side, hold = buffers
        patch = turns[index]
        row, col = place_of(patch)
        near, far = search_block(windows_ref, owners[patch])
        tile = first_ref[pl.ds(row, 128), pl.ds(col, 128)]
        spread_window(near, far, ahead, 0, (0, 22, 44))
        spread_template(tile, front, 0, 0, False)
        centre = flipped_centre(near, far)
        spread_template(centre.astype(jnp.bfloat16), back, 0, 0, True)
        around = flipped_around(beside_ref, row, col)
        spread_window(around[:, :128], around[:, 128:], behind, 0, (75, 53, 31))
        bad = jnp.float32(0.0)
        for place, values in enumerate((tile.astype(jnp.float32), centre)):
            mean, scale, large = level_of(values)
            side[2 * place : 2 * place + 1, :] = scale * mean
            side[2 * place + 1 : 2 * place + 2, :] = scale
            bad = jnp.maximum(bad, large)
        large_ref[0] = jnp.maximum(large_ref[0], bad.astype(jnp.int32))

    def sums(index, buffers):
        ahead, behind, front, back, side, hold = buffers
        one = multiplied(front, ahead)
        two = multiplied(back, behind)
        raw = side[1:2, :] * one[:count] + side[3:4, :] * two[:count]
        box = side[0:1, :] * one[count:] + side[2:3, :] * two[count:]
        for shift in (1, 2, 4, 8):
            box = box + pltpu.roll(box, 256 - shift, 1)
        patch = jnp.where(index < count_of[0], turns[jnp.minimum(index, 15)], 16)
        out_ref[patch] = fold_diagonals(raw, hold) - box[:24]

    build(0, scratch[:6])

    def pair(step, carry):
        sums(2 * step, scratch[:6])
        build(jnp.minimum(2 * step + 1, 15), scratch[6:])
        sums(2 * step + 1, scratch[6:])
        build(jnp.minimum(2 * step + 2, 15), scratch[:6])
        return carry

    lax.fori_loop(0, (count_of[0] + 1) // 2, pair, 0)


def surfaces_of(owners, turns, count_of, first, beside, windows, before=None):
    phase = int(before is not None)
    arrays = [first, beside, windows] + [before] * phase
    factors = [pltpu.VMEM((DEPTH, 256, 128), jnp.bfloat16)] * 2
    factors += [pltpu.VMEM((DEPTH, TALL, 128), jnp.bfloat16)] * 2
    sides = [pltpu.VMEM((8, 256), jnp.float32), pltpu.VMEM((2, 384, 128), jnp.float32)]
    return pl.pallas_call(
        functools.partial(surface_kernel, phase=phase),
        out_shape=[
            jax.ShapeDtypeStruct((17, 24, 256), jnp.float32),
            jax.ShapeDtypeStruct((1,), jnp.int32),
        ],
        in_specs=[pl.BlockSpec(memory_space=pltpu.SMEM)] * 3
        + [pl.BlockSpec(memory_space=pltpu.VMEM)] * len(arrays),
        out_specs=[
            pl.BlockSpec(memory_space=pltpu.VMEM),
            pl.BlockSpec(memory_space=pltpu.SMEM),
        ],
        scratch_shapes=(factors + sides) * 2,
        compiler_params=pltpu.CompilerParams(vmem_limit_bytes=32 * 1024 * 1024),
        cost_estimate=pl.CostEstimate(
            flops=20_000_000_000, bytes_accessed=8_000_000, transcendentals=0
        ),
        name=("surfaces_later" if phase else "surfaces_early"),
    )(owners, turns, count_of, *arrays)


def finish(folded, mask):
    parts = folded[:16, :COLS, : SPAN * BANDS].reshape(16, COLS, BANDS, SPAN)[..., :SHIFTS]
    surface = parts.transpose(0, 3, 2, 1).reshape(16, SHIFTS, BANDS * COLS)[:, :, :SHIFTS]
    scale = mask.reshape(16, 1).astype(jnp.float32) / (2.0 * SIDE)
    return surface.reshape(16, SHIFTS * SHIFTS) * scale


def moved(values, axis, forward):
    count = lax.axis_size(axis)
    pairs = [(i, i + 1) if forward else (i + 1, i) for i in range(count - 1)]
    return lax.ppermute(values, axis, pairs)


def rows_around(first, second):
    from_above = moved(jnp.concatenate([first[-HALO:], second[-HALO:]], 1), "band", True)
    from_below = moved(jnp.concatenate([first[:HALO], second[:HALO]], 1), "band", False)
    return from_above, from_below


def with_margins(first, second, from_above, from_below):
    width = first.shape[1]
    first = jnp.concatenate([from_above[:, :width], first, from_below[:, :width]], 0)
    second = jnp.concatenate([from_above[:, width:], second, from_below[:, width:]], 0)
    from_left = moved(jnp.concatenate([first[:, -HALO:], second[:, -HALO:]], 1), "strip", True)
    from_right = moved(jnp.concatenate([first[:, :HALO], second[:, :HALO]], 1), "strip", False)
    first = jnp.concatenate([from_left[:, :HALO], first, from_right[:, :HALO]], 1)
    second = jnp.concatenate([from_left[:, HALO:], second, from_right[:, HALO:]], 1)
    return first, second


def to_owners(values):
    return lax.all_to_all(values, "strip", split_axis=0, concat_axis=0, tiled=True)


def on_device(first, second, owner_strip, target_tile, offsets, valid_mask):
    strips = lax.axis_size("strip")
    from_above, from_below = rows_around(first, second)
    order = jnp.arange(16, dtype=jnp.int32)
    owners = owner_strip.reshape(16)
    earlier = (owners[:, None] == owners[None, :]) & (order[None, :] < order[:, None])
    later = jnp.sum(earlier.astype(jnp.int32), axis=1)
    slot_of = owners * 2 + later
    placing = (slot_of[:, None] == jnp.arange(2 * strips, dtype=jnp.int32)[None, :]).astype(jnp.int32)
    tiles = target_tile.reshape(16)
    shifts = offsets.reshape(16, 2)
    corner = jnp.stack(
        [tiles // 4 * SIDE + shifts[:, 0] + 32, tiles % 4 * SIDE + shifts[:, 1] + 32], axis=1
    )
    outgoing = jnp.sum(placing[:, :, None] * corner[:, None, :], axis=0).reshape(strips, 2, 2)
    outgoing, from_above, from_below = lax.optimization_barrier((outgoing, from_above, from_below))
    requests = to_owners(outgoing)
    beside, wide = with_margins(first, second, from_above, from_below)
    windows = [to_owners(cut_windows(wide, requests, place)) for place in range(2)]
    ahead = (later[None, :] < later[:, None]) | (
        (later[None, :] == later[:, None]) & (order[None, :] < order[:, None])
    )
    rank = jnp.sum(ahead.astype(jnp.int32), axis=1)
    late = jnp.sum(later).reshape(1)
    early = 16 - late
    turns, later_turns = [
        jnp.sum((rank[None, :] == (order + at)[:, None]).astype(jnp.int32) * order[None, :], axis=1)
        for at in (0, early)
    ]
    folded, large = surfaces_of(owners, turns, early, first, beside, windows[0])
    folded, larger = surfaces_of(owners, later_turns, late, first, beside, windows[1], folded)
    folded = lax.cond(
        jnp.maximum(large[0], larger[0]) > 0,
        lambda: careful_surfaces(owners, later, first, beside, *windows),
        lambda: folded,
    )
    return finish(folded, valid_mask).reshape(1, 1, 16, SHIFTS * SHIFTS)


def solution(mesh):
    return jax.shard_map(
        on_device,
        mesh=mesh,
        in_specs=(
            P("band", "strip"),
            P("band", "strip"),
            P("band", "strip", None, None),
            P("band", "strip", None),
            P("band", "strip", None, None),
            P("band", "strip", None),
        ),
        out_specs=P("band", "strip", None, None),
        check_vma=False,
    )
```

```python
import functools

import jax
import jax.numpy as jnp
from jax import lax
from jax.experimental import pallas as pl
from jax.experimental.pallas import tpu as pltpu
from jax.sharding import PartitionSpec as P

SIDE = 128
SHIFTS = 64
SEARCH = 192
HALO = 64
EPSILON = 1e-05
COLS = 22
BANDS = 3
ROWS = 16
SPAN = 80
BLOCKS = SIDE // ROWS
DEPTH = BLOCKS + 2
PACKED = SEARCH + SEARCH // 2
EXTRA = 32
TALL = COLS * ROWS + EXTRA
DIMS = (((1,), (1,)), ((), ()))


def lane_iota(shape):
    return lax.broadcasted_iota(jnp.int32, shape, len(shape) - 1)


def cut_kernel(requests, scene_ref, out_ref, wide, *, place):
    for part in range(5):
        wide[part] = scene_ref[:, 128 * part : 128 * (part + 1)].astype(jnp.float32)
    wide[5] = jnp.zeros((640, 128), jnp.float32)
    lanes = lane_iota((SEARCH, 128))
    lower = lane_iota((SEARCH // 2, 128)) < 64

    def one(slot, carry):
        top = requests[slot, place, 0]
        left = requests[slot, place, 1]
        base = left // 128
        rest = left % 128
        turn = (128 - rest) % 128
        turned = [
            pltpu.roll(wide[base + part, pl.ds(top, SEARCH), :], turn, 1) for part in range(3)
        ]
        inside = lanes < 128 - rest
        near = jnp.where(inside, turned[0], turned[1])
        far = jnp.where(inside, turned[1], turned[2])
        out_ref[slot, :SEARCH, :] = near.astype(jnp.bfloat16)
        half = SEARCH // 2
        mixed = jnp.where(lower, far[:half], pltpu.roll(far[half:], 64, 1))
        out_ref[slot, SEARCH:, :] = mixed.astype(jnp.bfloat16)
        return carry

    lax.fori_loop(0, out_ref.shape[0], one, 0)


def cut_windows(scene, requests, place):
    slots = requests.shape[0]
    return pl.pallas_call(
        functools.partial(cut_kernel, place=place),
        out_shape=jax.ShapeDtypeStruct((slots, PACKED, 128), jnp.bfloat16),
        in_specs=[
            pl.BlockSpec(memory_space=pltpu.SMEM),
            pl.BlockSpec(memory_space=pltpu.VMEM),
        ],
        out_specs=pl.BlockSpec(memory_space=pltpu.VMEM),
        scratch_shapes=[pltpu.VMEM((6, 640, 128), jnp.float32)],
        compiler_params=pltpu.CompilerParams(vmem_limit_bytes=32 * 1024 * 1024),
        name="cut_windows",
    )(requests, scene)


def normalize(patch):
    centered = patch - jnp.mean(patch)
    return centered * lax.rsqrt(jnp.mean(centered * centered) + EPSILON)


def exchange(size):
    rows = lax.broadcasted_iota(jnp.int32, (size, size), 0)
    return (rows + lane_iota((size, size)) == size - 1).astype(jnp.bfloat16)


def halves(values):
    high = values.astype(jnp.bfloat16)
    low = (values - high.astype(jnp.float32)).astype(jnp.bfloat16)
    return high, low


def spread_template(values, left, row_at, lane_at, reverse):
    lanes = lane_iota((ROWS, 128)).astype(jnp.int16)
    groups = (lane_iota((ROWS, 128)) // 32).astype(jnp.int16)
    within = (lane_iota((ROWS, 128)) % 32).astype(jnp.int16)
    zero = jnp.zeros((ROWS, 128), jnp.bfloat16)
    blocks = [values[ROWS * q : ROWS * (q + 1)] for q in range(BLOCKS)]
    ends = []
    for group in range(2):
        end = zero
        for part in range(4):
            turned = pltpu.roll(blocks[4 * group + part], 32 * part, 1)
            end = jnp.where(groups == (part + 3) % 4, turned, end)
        ends.append(end)
    for a in range(COLS):
        shift = COLS - 1 - a if reverse else a
        rows = pl.ds(row_at + ROWS * a, ROWS)
        for q in range(BLOCKS):
            moved = pltpu.roll(blocks[q], shift, 1)
            moved = jnp.where(lanes >= shift, moved, zero)
            left[lane_at + q, rows] = moved
        for group in range(2):
            moved = pltpu.roll(ends[group], shift, 1)
            moved = jnp.where(within < shift, moved, zero)
            left[lane_at + BLOCKS + group, rows] = moved


def spread_window(near, far, right, lane_at, offsets):
    lanes = lane_iota((SEARCH, 128)).astype(jnp.int16)
    for b, offset in enumerate(offsets):
        back = (128 - offset) % 128
        main = near
        if offset:
            main = jnp.where(
                lanes < 128 - offset, pltpu.roll(near, back, 1), pltpu.roll(far, back, 1)
            )
        rows = pl.ds(SPAN * b, SPAN)
        for q in range(BLOCKS):
            right[lane_at + q, rows] = main[ROWS * q : ROWS * q + SPAN]
        turned = [pltpu.roll(far, (back + 32 * part) % 128, 1) for part in range(4)]
        few = (lane_iota((SPAN, 128)) // 32).astype(jnp.int16)
        for group in range(2):
            tail = turned[0][ROWS * 4 * group : ROWS * 4 * group + SPAN]
            for part in range(1, 4):
                q = 4 * group + part
                tail = jnp.where(few == part, turned[part][ROWS * q : ROWS * q + SPAN], tail)
            right[lane_at + BLOCKS + group, rows] = tail


def fold_diagonals(product, hold):
    for half in range(2):
        hold[half, : COLS * ROWS] = product[:, 128 * half : 128 * (half + 1)]
    groups = []
    for group in range(3):
        terms = [
            jnp.concatenate(
                [hold[half, pl.ds(128 * group + p, 8, stride=ROWS), :] for half in range(2)], axis=1
            )
            for p in range(ROWS)
        ]
        for step in (8, 4, 2, 1):
            terms = [terms[p] + pltpu.roll(terms[p + step], 256 - step, 1) for p in range(step)]
        groups.append(terms[0])
    return jnp.concatenate(groups, axis=0)


def multiplied(left, right):
    factors = [
        jnp.concatenate([side[block] for block in range(side.shape[0])], axis=1)
        for side in (left, right)
    ]
    return lax.dot_general(*factors, DIMS, preferred_element_type=jnp.float32)


def search_block(windows_ref, slot):
    near = windows_ref[slot, :SEARCH, :]
    packed = windows_ref[slot, SEARCH:, :]
    return near, jnp.concatenate([packed, pltpu.roll(packed, 64, 1)], axis=0)


def flipped_centre(near, far):
    flip = exchange(128)
    low, high = [
        jnp.dot(flip, part[32:160], preferred_element_type=jnp.float32) for part in (near, far)
    ]
    lanes = lane_iota((128, 128))
    return jnp.where(lanes < 96, pltpu.roll(low, 96, 1), pltpu.roll(high, 96, 1))


def flipped_around(beside_ref, row, col):
    return jnp.dot(
        exchange(SEARCH),
        beside_ref[pl.ds(row + 32, SEARCH), pl.ds(col, 256)],
        preferred_element_type=jnp.float32,
    ).astype(jnp.bfloat16)


def place_of(patch):
    return pl.multiple_of(patch // 4 * 128, 128), pl.multiple_of(patch % 4 * 128, 128)


def careful_kernel(owners, later, first_ref, beside_ref, windows_ref, others_ref, out_ref, left, right, hold):
    right[:, SPAN * BANDS :] = jnp.zeros((2 * DEPTH, 256 - SPAN * BANDS, 128), jnp.bfloat16)
    count = COLS * ROWS

    hold[:, count:] = jnp.zeros((2, 32, 128), jnp.float32)
    out_ref[16] = jnp.zeros((24, 256), jnp.float32)

    def one(patch, carry):
        row, col = place_of(patch)
        near, far = [
            jnp.where(later[patch] > 0, other, one)
            for one, other in zip(
                search_block(windows_ref, owners[patch]), search_block(others_ref, owners[patch])
            )
        ]
        template = normalize(first_ref[pl.ds(row, 128), pl.ds(col, 128)].astype(jnp.float32))
        centre = flipped_centre(near, far)
        around = flipped_around(beside_ref, row, col)
        inner = first_ref[pl.ds(row, 128), pl.ds(col, 128)].astype(jnp.float32)
        sides = ((template, jnp.mean(centre), False), (normalize(centre), jnp.mean(inner), True))
        rest = jnp.float32(0.0)
        for place, (values, level, reverse) in enumerate(sides):
            high, low = halves(values)
            for half, piece in enumerate((high, low)):
                spread_template(piece, left, count * half, DEPTH * place, reverse)
            rest += level * (
                jnp.sum(high.astype(jnp.float32)) + jnp.sum(low.astype(jnp.float32))
            )
        spread_window(near, far, right, 0, (0, 22, 44))
        spread_window(around[:, :128], around[:, 128:], right, DEPTH, (75, 53, 31))
        both = multiplied(left, right)
        out_ref[patch] = fold_diagonals(both[:count] + both[count:], hold) - rest
        return carry

    lax.fori_loop(0, 16, one, 0)


def careful_surfaces(owners, later, first, beside, windows, others):
    return pl.pallas_call(
        careful_kernel,
        out_shape=jax.ShapeDtypeStruct((17, 24, 256), jnp.float32),
        in_specs=[pl.BlockSpec(memory_space=pltpu.SMEM)] * 2
        + [pl.BlockSpec(memory_space=pltpu.VMEM)] * 4,
        out_specs=pl.BlockSpec(memory_space=pltpu.VMEM),
        scratch_shapes=[
            pltpu.VMEM((2 * DEPTH, 2 * COLS * ROWS, 128), jnp.bfloat16),
            pltpu.VMEM((2 * DEPTH, 256, 128), jnp.bfloat16),
            pltpu.VMEM((2, 384, 128), jnp.float32),
        ],
        compiler_params=pltpu.CompilerParams(vmem_limit_bytes=40 * 1024 * 1024),
        name="careful_surfaces",
    )(owners, later, first, beside, windows, others)


def ones_rows(left, reverse):
    index = lax.broadcasted_iota(jnp.int32, (EXTRA, 128), 0)
    lanes = lane_iota((EXTRA, 128))
    shift = COLS - 1 - index if reverse else index
    main = jnp.where((index < COLS) & (lanes >= shift), 1.0, 0.0).astype(jnp.bfloat16)
    tail = jnp.where((index < COLS) & (lanes % 32 < shift), 1.0, 0.0).astype(jnp.bfloat16)
    for q in range(BLOCKS):
        left[q, COLS * ROWS :] = main
    for group in range(2):
        left[BLOCKS + group, COLS * ROWS :] = tail


def level_of(values):
    mean = jnp.mean(values)
    centered = values - mean
    spread = jnp.mean(centered * centered)
    large = jnp.where(mean * mean > 4.0 * spread, 1.0, 0.0)
    return mean, lax.rsqrt(jnp.full((1, 256), spread + EPSILON)), large


def surface_kernel(
    owners, turns, count_of, first_ref, beside_ref, windows_ref, *rest, phase
):
    before, (out_ref, large_ref, *scratch) = (rest[0], rest[1:]) if phase else (None, rest)
    count = COLS * ROWS
    large_ref[0] = 0
    if phase:
        out_ref[...] = before[...]
    for ahead, behind, front, back, side, hold in (scratch[:6], scratch[6:]):
        hold[:, count:] = jnp.zeros((2, 32, 128), jnp.float32)
        ones_rows(front, False)
        ones_rows(back, True)
        for right in (ahead, behind):
            right[:, SPAN * BANDS :] = jnp.zeros((DEPTH, 256 - SPAN * BANDS, 128), jnp.bfloat16)

    def build(index, buffers):
        ahead, behind, front, back, side, hold = buffers
        patch = turns[index]
        row, col = place_of(patch)
        near, far = search_block(windows_ref, owners[patch])
        tile = first_ref[pl.ds(row, 128), pl.ds(col, 128)]
        spread_window(near, far, ahead, 0, (0, 22, 44))
        spread_template(tile, front, 0, 0, False)
        centre = flipped_centre(near, far)
        spread_template(centre.astype(jnp.bfloat16), back, 0, 0, True)
        around = flipped_around(beside_ref, row, col)
        spread_window(around[:, :128], around[:, 128:], behind, 0, (75, 53, 31))
        bad = jnp.float32(0.0)
        for place, values in enumerate((tile.astype(jnp.float32), centre)):
            mean, scale, large = level_of(values)
            side[2 * place : 2 * place + 1, :] = scale * mean
            side[2 * place + 1 : 2 * place + 2, :] = scale
            bad = jnp.maximum(bad, large)
        large_ref[0] = jnp.maximum(large_ref[0], bad.astype(jnp.int32))

    def sums(index, buffers):
        ahead, behind, front, back, side, hold = buffers
        one = multiplied(front, ahead)
        two = multiplied(back, behind)
        raw = side[1:2, :] * one[:count] + side[3:4, :] * two[:count]
        box = side[0:1, :] * one[count:] + side[2:3, :] * two[count:]
        for shift in (1, 2, 4, 8):
            box = box + pltpu.roll(box, 256 - shift, 1)
        patch = jnp.where(index < count_of[0], turns[jnp.minimum(index, 15)], 16)
        out_ref[patch] = fold_diagonals(raw, hold) - box[:24]

    build(0, scratch[:6])

    def pair(step, carry):
        sums(2 * step, scratch[:6])
        build(jnp.minimum(2 * step + 1, 15), scratch[6:])
        sums(2 * step + 1, scratch[6:])
        build(jnp.minimum(2 * step + 2, 15), scratch[:6])
        return carry

    lax.fori_loop(0, (count_of[0] + 1) // 2, pair, 0)


def surfaces_of(owners, turns, count_of, first, beside, windows, before=None):
    phase = int(before is not None)
    arrays = [first, beside, windows] + [before] * phase
    factors = [pltpu.VMEM((DEPTH, 256, 128), jnp.bfloat16)] * 2
    factors += [pltpu.VMEM((DEPTH, TALL, 128), jnp.bfloat16)] * 2
    sides = [pltpu.VMEM((8, 256), jnp.float32), pltpu.VMEM((2, 384, 128), jnp.float32)]
    return pl.pallas_call(
        functools.partial(surface_kernel, phase=phase),
        out_shape=[
            jax.ShapeDtypeStruct((17, 24, 256), jnp.float32),
            jax.ShapeDtypeStruct((1,), jnp.int32),
        ],
        in_specs=[pl.BlockSpec(memory_space=pltpu.SMEM)] * 3
        + [pl.BlockSpec(memory_space=pltpu.VMEM)] * len(arrays),
        out_specs=[
            pl.BlockSpec(memory_space=pltpu.VMEM),
            pl.BlockSpec(memory_space=pltpu.SMEM),
        ],
        scratch_shapes=(factors + sides) * 2,
        compiler_params=pltpu.CompilerParams(vmem_limit_bytes=32 * 1024 * 1024),
        cost_estimate=pl.CostEstimate(
            flops=20_000_000_000, bytes_accessed=8_000_000, transcendentals=0
        ),
        name=("surfaces_later" if phase else "surfaces_early"),
    )(owners, turns, count_of, *arrays)


def finish(folded, mask):
    parts = folded[:16, :COLS, : SPAN * BANDS].reshape(16, COLS, BANDS, SPAN)[..., :SHIFTS]
    surface = parts.transpose(0, 3, 2, 1).reshape(16, SHIFTS, BANDS * COLS)[:, :, :SHIFTS]
    scale = mask.reshape(16, 1).astype(jnp.float32) / (2.0 * SIDE)
    return surface.reshape(16, SHIFTS * SHIFTS) * scale


def moved(values, axis, forward):
    count = lax.axis_size(axis)
    pairs = [(i, i + 1) if forward else (i + 1, i) for i in range(count - 1)]
    return lax.ppermute(values, axis, pairs)


def rows_around(first, second):
    from_above = moved(jnp.concatenate([first[-HALO:], second[-HALO:]], 1), "band", True)
    from_below = moved(jnp.concatenate([first[:HALO], second[:HALO]], 1), "band", False)
    return from_above, from_below


def with_margins(first, second, from_above, from_below):
    width = first.shape[1]
    first = jnp.concatenate([from_above[:, :width], first, from_below[:, :width]], 0)
    second = jnp.concatenate([from_above[:, width:], second, from_below[:, width:]], 0)
    from_left = moved(jnp.concatenate([first[:, -HALO:], second[:, -HALO:]], 1), "strip", True)
    from_right = moved(jnp.concatenate([first[:, :HALO], second[:, :HALO]], 1), "strip", False)
    first = jnp.concatenate([from_left[:, :HALO], first, from_right[:, :HALO]], 1)
    second = jnp.concatenate([from_left[:, HALO:], second, from_right[:, HALO:]], 1)
    return first, second


def to_owners(values):
    return lax.all_to_all(values, "strip", split_axis=0, concat_axis=0, tiled=True)


def on_device(first, second, owner_strip, target_tile, offsets, valid_mask):
    strips = lax.axis_size("strip")
    from_above, from_below = rows_around(first, second)
    order = jnp.arange(16, dtype=jnp.int32)
    owners = owner_strip.reshape(16)
    earlier = (owners[:, None] == owners[None, :]) & (order[None, :] < order[:, None])
    later = jnp.sum(earlier.astype(jnp.int32), axis=1)
    slot_of = owners * 2 + later
    placing = (slot_of[:, None] == jnp.arange(2 * strips, dtype=jnp.int32)[None, :]).astype(jnp.int32)
    tiles = target_tile.reshape(16)
    shifts = offsets.reshape(16, 2)
    corner = jnp.stack(
        [tiles // 4 * SIDE + shifts[:, 0] + 32, tiles % 4 * SIDE + shifts[:, 1] + 32], axis=1
    )
    outgoing = jnp.sum(placing[:, :, None] * corner[:, None, :], axis=0).reshape(strips, 2, 2)
    requests = to_owners(jnp.pad(outgoing, ((0, 0), (0, 22), (0, 126))))[:, :2, :2]
    beside, wide = with_margins(first, second, from_above, from_below)
    windows = [to_owners(cut_windows(wide, requests, place)) for place in range(2)]
    ahead = (later[None, :] < later[:, None]) | (
        (later[None, :] == later[:, None]) & (order[None, :] < order[:, None])
    )
    rank = jnp.sum(ahead.astype(jnp.int32), axis=1)
    late = jnp.sum(later).reshape(1)
    early = 16 - late
    turns, later_turns = [
        jnp.sum((rank[None, :] == (order + at)[:, None]).astype(jnp.int32) * order[None, :], axis=1)
        for at in (0, early)
    ]
    folded, large = surfaces_of(owners, turns, early, first, beside, windows[0])
    folded, larger = surfaces_of(owners, later_turns, late, first, beside, windows[1], folded)
    folded = lax.cond(
        jnp.maximum(large[0], larger[0]) > 0,
        lambda: careful_surfaces(owners, later, first, beside, *windows),
        lambda: folded,
    )
    return finish(folded, valid_mask).reshape(1, 1, 16, SHIFTS * SHIFTS)


def solution(mesh):
    return jax.shard_map(
        on_device,
        mesh=mesh,
        in_specs=(
            P("band", "strip"),
            P("band", "strip"),
            P("band", "strip", None, None),
            P("band", "strip", None),
            P("band", "strip", None, None),
            P("band", "strip", None),
        ),
        out_specs=P("band", "strip", None, None),
        check_vma=False,
    )
```

```python
import functools

import jax
import jax.numpy as jnp
from jax import lax
from jax.experimental import pallas as pl
from jax.experimental.pallas import tpu as pltpu
from jax.sharding import PartitionSpec as P

SIDE = 128
SHIFTS = 64
SEARCH = 192
HALO = 64
EPSILON = 1e-05
COLS = 22
BANDS = 3
ROWS = 16
SPAN = 80
BLOCKS = SIDE // ROWS
DEPTH = BLOCKS + 2
PACKED = SEARCH + SEARCH // 2
EXTRA = 32
TALL = COLS * ROWS + EXTRA
DIMS = (((1,), (1,)), ((), ()))


def lane_iota(shape):
    return lax.broadcasted_iota(jnp.int32, shape, len(shape) - 1)


def cut_kernel(requests, scene_ref, out_ref, wide, *, place):
    for part in range(5):
        wide[part] = scene_ref[:, 128 * part : 128 * (part + 1)].astype(jnp.float32)
    wide[5] = jnp.zeros((640, 128), jnp.float32)
    lanes = lane_iota((SEARCH, 128))
    lower = lane_iota((SEARCH // 2, 128)) < 64

    def one(slot, carry):
        top = requests[slot, place, 0]
        left = requests[slot, place, 1]
        base = left // 128
        rest = left % 128
        turn = (128 - rest) % 128
        turned = [
            pltpu.roll(wide[base + part, pl.ds(top, SEARCH), :], turn, 1) for part in range(3)
        ]
        inside = lanes < 128 - rest
        near = jnp.where(inside, turned[0], turned[1])
        far = jnp.where(inside, turned[1], turned[2])
        out_ref[slot, :SEARCH, :] = near.astype(jnp.bfloat16)
        half = SEARCH // 2
        mixed = jnp.where(lower, far[:half], pltpu.roll(far[half:], 64, 1))
        out_ref[slot, SEARCH:, :] = mixed.astype(jnp.bfloat16)
        return carry

    lax.fori_loop(0, out_ref.shape[0], one, 0)


def cut_windows(scene, requests, place):
    slots = requests.shape[0]
    return pl.pallas_call(
        functools.partial(cut_kernel, place=place),
        out_shape=jax.ShapeDtypeStruct((slots, PACKED, 128), jnp.bfloat16),
        in_specs=[
            pl.BlockSpec(memory_space=pltpu.SMEM),
            pl.BlockSpec(memory_space=pltpu.VMEM),
        ],
        out_specs=pl.BlockSpec(memory_space=pltpu.VMEM),
        scratch_shapes=[pltpu.VMEM((6, 640, 128), jnp.float32)],
        compiler_params=pltpu.CompilerParams(vmem_limit_bytes=32 * 1024 * 1024),
        name="cut_windows",
    )(requests, scene)


def normalize(patch):
    centered = patch - jnp.mean(patch)
    return centered * lax.rsqrt(jnp.mean(centered * centered) + EPSILON)


def exchange(size):
    rows = lax.broadcasted_iota(jnp.int32, (size, size), 0)
    return (rows + lane_iota((size, size)) == size - 1).astype(jnp.bfloat16)


def halves(values):
    high = values.astype(jnp.bfloat16)
    low = (values - high.astype(jnp.float32)).astype(jnp.bfloat16)
    return high, low


def spread_template(values, left, row_at, lane_at, reverse):
    lanes = lane_iota((ROWS, 128)).astype(jnp.int16)
    groups = (lane_iota((ROWS, 128)) // 32).astype(jnp.int16)
    within = (lane_iota((ROWS, 128)) % 32).astype(jnp.int16)
    zero = jnp.zeros((ROWS, 128), jnp.bfloat16)
    blocks = [values[ROWS * q : ROWS * (q + 1)] for q in range(BLOCKS)]
    ends = []
    for group in range(2):
        end = zero
        for part in range(4):
            turned = pltpu.roll(blocks[4 * group + part], 32 * part, 1)
            end = jnp.where(groups == (part + 3) % 4, turned, end)
        ends.append(end)
    for a in range(COLS):
        shift = COLS - 1 - a if reverse else a
        rows = pl.ds(row_at + ROWS * a, ROWS)
        for q in range(BLOCKS):
            moved = pltpu.roll(blocks[q], shift, 1)
            moved = jnp.where(lanes >= shift, moved, zero)
            left[lane_at + q, rows] = moved
        for group in range(2):
            moved = pltpu.roll(ends[group], shift, 1)
            moved = jnp.where(within < shift, moved, zero)
            left[lane_at + BLOCKS + group, rows] = moved


def spread_window(near, far, right, lane_at, offsets):
    lanes = lane_iota((SEARCH, 128)).astype(jnp.int16)
    for b, offset in enumerate(offsets):
        back = (128 - offset) % 128
        main = near
        if offset:
            main = jnp.where(
                lanes < 128 - offset, pltpu.roll(near, back, 1), pltpu.roll(far, back, 1)
            )
        rows = pl.ds(SPAN * b, SPAN)
        for q in range(BLOCKS):
            right[lane_at + q, rows] = main[ROWS * q : ROWS * q + SPAN]
        turned = [pltpu.roll(far, (back + 32 * part) % 128, 1) for part in range(4)]
        few = (lane_iota((SPAN, 128)) // 32).astype(jnp.int16)
        for group in range(2):
            tail = turned[0][ROWS * 4 * group : ROWS * 4 * group + SPAN]
            for part in range(1, 4):
                q = 4 * group + part
                tail = jnp.where(few == part, turned[part][ROWS * q : ROWS * q + SPAN], tail)
            right[lane_at + BLOCKS + group, rows] = tail


def fold_diagonals(product, hold):
    for half in range(2):
        hold[half, : COLS * ROWS] = product[:, 128 * half : 128 * (half + 1)]
    groups = []
    for group in range(3):
        terms = [
            jnp.concatenate(
                [hold[half, pl.ds(128 * group + p, 8, stride=ROWS), :] for half in range(2)], axis=1
            )
            for p in range(ROWS)
        ]
        for step in (8, 4, 2, 1):
            terms = [terms[p] + pltpu.roll(terms[p + step], 256 - step, 1) for p in range(step)]
        groups.append(terms[0])
    return jnp.concatenate(groups, axis=0)


def multiplied(left, right):
    factors = [
        jnp.concatenate([side[block] for block in range(side.shape[0])], axis=1)
        for side in (left, right)
    ]
    return lax.dot_general(*factors, DIMS, preferred_element_type=jnp.float32)


def search_block(windows_ref, slot):
    near = windows_ref[slot, :SEARCH, :]
    packed = windows_ref[slot, SEARCH:, :]
    return near, jnp.concatenate([packed, pltpu.roll(packed, 64, 1)], axis=0)


def flipped_centre(near, far):
    flip = exchange(128)
    low, high = [
        jnp.dot(flip, part[32:160], preferred_element_type=jnp.float32) for part in (near, far)
    ]
    lanes = lane_iota((128, 128))
    return jnp.where(lanes < 96, pltpu.roll(low, 96, 1), pltpu.roll(high, 96, 1))


def flipped_around(beside_ref, row, col):
    return jnp.dot(
        exchange(SEARCH),
        beside_ref[pl.ds(row + 32, SEARCH), pl.ds(col, 256)],
        preferred_element_type=jnp.float32,
    ).astype(jnp.bfloat16)


def place_of(patch):
    return pl.multiple_of(patch // 4 * 128, 128), pl.multiple_of(patch % 4 * 128, 128)


def careful_kernel(owners, later, first_ref, beside_ref, windows_ref, others_ref, out_ref, left, right, hold):
    right[:, SPAN * BANDS :] = jnp.zeros((2 * DEPTH, 256 - SPAN * BANDS, 128), jnp.bfloat16)
    count = COLS * ROWS

    hold[:, count:] = jnp.zeros((2, 32, 128), jnp.float32)
    out_ref[16] = jnp.zeros((24, 256), jnp.float32)

    def one(patch, carry):
        row, col = place_of(patch)
        near, far = [
            jnp.where(later[patch] > 0, other, one)
            for one, other in zip(
                search_block(windows_ref, owners[patch]), search_block(others_ref, owners[patch])
            )
        ]
        template = normalize(first_ref[pl.ds(row, 128), pl.ds(col, 128)].astype(jnp.float32))
        centre = flipped_centre(near, far)
        around = flipped_around(beside_ref, row, col)
        inner = first_ref[pl.ds(row, 128), pl.ds(col, 128)].astype(jnp.float32)
        sides = ((template, jnp.mean(centre), False), (normalize(centre), jnp.mean(inner), True))
        rest = jnp.float32(0.0)
        for place, (values, level, reverse) in enumerate(sides):
            high, low = halves(values)
            for half, piece in enumerate((high, low)):
                spread_template(piece, left, count * half, DEPTH * place, reverse)
            rest += level * (
                jnp.sum(high.astype(jnp.float32)) + jnp.sum(low.astype(jnp.float32))
            )
        spread_window(near, far, right, 0, (0, 22, 44))
        spread_window(around[:, :128], around[:, 128:], right, DEPTH, (75, 53, 31))
        both = multiplied(left, right)
        out_ref[patch] = fold_diagonals(both[:count] + both[count:], hold) - rest
        return carry

    lax.fori_loop(0, 16, one, 0)


def careful_surfaces(owners, later, first, beside, windows, others):
    return pl.pallas_call(
        careful_kernel,
        out_shape=jax.ShapeDtypeStruct((17, 24, 256), jnp.float32),
        in_specs=[pl.BlockSpec(memory_space=pltpu.SMEM)] * 2
        + [pl.BlockSpec(memory_space=pltpu.VMEM)] * 4,
        out_specs=pl.BlockSpec(memory_space=pltpu.VMEM),
        scratch_shapes=[
            pltpu.VMEM((2 * DEPTH, 2 * COLS * ROWS, 128), jnp.bfloat16),
            pltpu.VMEM((2 * DEPTH, 256, 128), jnp.bfloat16),
            pltpu.VMEM((2, 384, 128), jnp.float32),
        ],
        compiler_params=pltpu.CompilerParams(vmem_limit_bytes=40 * 1024 * 1024),
        name="careful_surfaces",
    )(owners, later, first, beside, windows, others)


def ones_rows(left, reverse):
    index = lax.broadcasted_iota(jnp.int32, (EXTRA, 128), 0)
    lanes = lane_iota((EXTRA, 128))
    shift = COLS - 1 - index if reverse else index
    main = jnp.where((index < COLS) & (lanes >= shift), 1.0, 0.0).astype(jnp.bfloat16)
    tail = jnp.where((index < COLS) & (lanes % 32 < shift), 1.0, 0.0).astype(jnp.bfloat16)
    for q in range(BLOCKS):
        left[q, COLS * ROWS :] = main
    for group in range(2):
        left[BLOCKS + group, COLS * ROWS :] = tail


def level_of(values):
    mean = jnp.mean(values)
    centered = values - mean
    spread = jnp.mean(centered * centered)
    large = jnp.where(mean * mean > 4.0 * spread, 1.0, 0.0)
    return mean, lax.rsqrt(jnp.full((1, 256), spread + EPSILON)), large


def surface_kernel(
    owners, turns, count_of, first_ref, beside_ref, windows_ref, *rest, phase
):
    before, (out_ref, large_ref, *scratch) = (rest[0], rest[1:]) if phase else (None, rest)
    count = COLS * ROWS
    large_ref[0] = 0
    if phase:
        out_ref[...] = before[...]
    for ahead, behind, front, back, side, hold in (scratch[:6], scratch[6:]):
        hold[:, count:] = jnp.zeros((2, 32, 128), jnp.float32)
        ones_rows(front, False)
        ones_rows(back, True)
        for right in (ahead, behind):
            right[:, SPAN * BANDS :] = jnp.zeros((DEPTH, 256 - SPAN * BANDS, 128), jnp.bfloat16)

    def build(index, buffers):
        ahead, behind, front, back, side, hold = buffers
        patch = turns[index]
        row, col = place_of(patch)
        near, far = search_block(windows_ref, owners[patch])
        tile = first_ref[pl.ds(row, 128), pl.ds(col, 128)]
        spread_window(near, far, ahead, 0, (0, 22, 44))
        spread_template(tile, front, 0, 0, False)
        centre = flipped_centre(near, far)
        spread_template(centre.astype(jnp.bfloat16), back, 0, 0, True)
        around = flipped_around(beside_ref, row, col)
        spread_window(around[:, :128], around[:, 128:], behind, 0, (75, 53, 31))
        bad = jnp.float32(0.0)
        for place, values in enumerate((tile.astype(jnp.float32), centre)):
            mean, scale, large = level_of(values)
            side[2 * place : 2 * place + 1, :] = scale * mean
            side[2 * place + 1 : 2 * place + 2, :] = scale
            bad = jnp.maximum(bad, large)
        large_ref[0] = jnp.maximum(large_ref[0], bad.astype(jnp.int32))

    def sums(index, buffers):
        ahead, behind, front, back, side, hold = buffers
        one = multiplied(front, ahead)
        two = multiplied(back, behind)
        raw = side[1:2, :] * one[:count] + side[3:4, :] * two[:count]
        box = side[0:1, :] * one[count:] + side[2:3, :] * two[count:]
        for shift in (1, 2, 4, 8):
            box = box + pltpu.roll(box, 256 - shift, 1)
        patch = jnp.where(index < count_of[0], turns[jnp.minimum(index, 15)], 16)
        out_ref[patch] = fold_diagonals(raw, hold) - box[:24]

    build(0, scratch[:6])

    def pair(step, carry):
        sums(2 * step, scratch[:6])
        build(jnp.minimum(2 * step + 1, 15), scratch[6:])
        sums(2 * step + 1, scratch[6:])
        build(jnp.minimum(2 * step + 2, 15), scratch[:6])
        return carry

    total = count_of[0]
    lax.fori_loop(0, jnp.maximum(total - 1, 0) // 2, pair, 0)

    @pl.when((total > 0) & (total % 2 == 0))
    def _():
        sums(total - 2, scratch[:6])
        build(total - 1, scratch[6:])
        sums(total - 1, scratch[6:])

    @pl.when(total % 2 == 1)
    def _():
        sums(total - 1, scratch[:6])


def surfaces_of(owners, turns, count_of, first, beside, windows, before=None):
    phase = int(before is not None)
    arrays = [first, beside, windows] + [before] * phase
    factors = [pltpu.VMEM((DEPTH, 256, 128), jnp.bfloat16)] * 2
    factors += [pltpu.VMEM((DEPTH, TALL, 128), jnp.bfloat16)] * 2
    sides = [pltpu.VMEM((8, 256), jnp.float32), pltpu.VMEM((2, 384, 128), jnp.float32)]
    return pl.pallas_call(
        functools.partial(surface_kernel, phase=phase),
        out_shape=[
            jax.ShapeDtypeStruct((17, 24, 256), jnp.float32),
            jax.ShapeDtypeStruct((1,), jnp.int32),
        ],
        in_specs=[pl.BlockSpec(memory_space=pltpu.SMEM)] * 3
        + [pl.BlockSpec(memory_space=pltpu.VMEM)] * len(arrays),
        out_specs=[
            pl.BlockSpec(memory_space=pltpu.VMEM),
            pl.BlockSpec(memory_space=pltpu.SMEM),
        ],
        scratch_shapes=(factors + sides) * 2,
        compiler_params=pltpu.CompilerParams(vmem_limit_bytes=32 * 1024 * 1024),
        cost_estimate=pl.CostEstimate(
            flops=20_000_000_000, bytes_accessed=8_000_000, transcendentals=0
        ),
        name=("surfaces_later" if phase else "surfaces_early"),
    )(owners, turns, count_of, *arrays)


def finish(folded, mask):
    parts = folded[:16, :COLS, : SPAN * BANDS].reshape(16, COLS, BANDS, SPAN)[..., :SHIFTS]
    surface = parts.transpose(0, 3, 2, 1).reshape(16, SHIFTS, BANDS * COLS)[:, :, :SHIFTS]
    scale = mask.reshape(16, 1).astype(jnp.float32) / (2.0 * SIDE)
    return surface.reshape(16, SHIFTS * SHIFTS) * scale


def moved(values, axis, forward):
    count = lax.axis_size(axis)
    pairs = [(i, i + 1) if forward else (i + 1, i) for i in range(count - 1)]
    return lax.ppermute(values, axis, pairs)


def rows_around(first, second):
    from_above = moved(jnp.concatenate([first[-HALO:], second[-HALO:]], 1), "band", True)
    from_below = moved(jnp.concatenate([first[:HALO], second[:HALO]], 1), "band", False)
    return from_above, from_below


def with_margins(first, second, from_above, from_below):
    width = first.shape[1]
    first = jnp.concatenate([from_above[:, :width], first, from_below[:, :width]], 0)
    second = jnp.concatenate([from_above[:, width:], second, from_below[:, width:]], 0)
    from_left = moved(jnp.concatenate([first[:, -HALO:], second[:, -HALO:]], 1), "strip", True)
    from_right = moved(jnp.concatenate([first[:, :HALO], second[:, :HALO]], 1), "strip", False)
    first = jnp.concatenate([from_left[:, :HALO], first, from_right[:, :HALO]], 1)
    second = jnp.concatenate([from_left[:, HALO:], second, from_right[:, HALO:]], 1)
    return first, second


def to_owners(values):
    return lax.all_to_all(values, "strip", split_axis=0, concat_axis=0, tiled=True)


def on_device(first, second, owner_strip, target_tile, offsets, valid_mask):
    strips = lax.axis_size("strip")
    from_above, from_below = rows_around(first, second)
    order = jnp.arange(16, dtype=jnp.int32)
    owners = owner_strip.reshape(16)
    earlier = (owners[:, None] == owners[None, :]) & (order[None, :] < order[:, None])
    later = jnp.sum(earlier.astype(jnp.int32), axis=1)
    slot_of = owners * 2 + later
    placing = (slot_of[:, None] == jnp.arange(2 * strips, dtype=jnp.int32)[None, :]).astype(jnp.int32)
    tiles = target_tile.reshape(16)
    shifts = offsets.reshape(16, 2)
    corner = jnp.stack(
        [tiles // 4 * SIDE + shifts[:, 0] + 32, tiles % 4 * SIDE + shifts[:, 1] + 32], axis=1
    )
    outgoing = jnp.sum(placing[:, :, None] * corner[:, None, :], axis=0).reshape(strips, 2, 2)
    outgoing, from_above, from_below = lax.optimization_barrier((outgoing, from_above, from_below))
    requests = to_owners(outgoing)
    beside, wide = with_margins(first, second, from_above, from_below)
    windows = [to_owners(cut_windows(wide, requests, place)) for place in range(2)]
    ahead = (later[None, :] < later[:, None]) | (
        (later[None, :] == later[:, None]) & (order[None, :] < order[:, None])
    )
    rank = jnp.sum(ahead.astype(jnp.int32), axis=1)
    late = jnp.sum(later).reshape(1)
    early = 16 - late
    turns, later_turns = [
        jnp.sum((rank[None, :] == (order + at)[:, None]).astype(jnp.int32) * order[None, :], axis=1)
        for at in (0, early)
    ]
    folded, large = surfaces_of(owners, turns, early, first, beside, windows[0])
    folded, larger = surfaces_of(owners, later_turns, late, first, beside, windows[1], folded)
    folded = lax.cond(
        jnp.maximum(large[0], larger[0]) > 0,
        lambda: careful_surfaces(owners, later, first, beside, *windows),
        lambda: folded,
    )
    return finish(folded, valid_mask).reshape(1, 1, 16, SHIFTS * SHIFTS)


def solution(mesh):
    return jax.shard_map(
        on_device,
        mesh=mesh,
        in_specs=(
            P("band", "strip"),
            P("band", "strip"),
            P("band", "strip", None, None),
            P("band", "strip", None),
            P("band", "strip", None, None),
            P("band", "strip", None),
        ),
        out_specs=P("band", "strip", None, None),
        check_vma=False,
    )
```
